32 devices in a mesh: ep: 16 (over z, y, x), dp: 2 (over core).
Axes of the slice: x: 2, y: 2, z: 4, core: 2. Of those that a mesh axis runs over, the one named last changes fastest.
Arguments:
- attention_out: bfloat16 [2048, 2560], P(('ep', 'dp')), may hold values from -6 to 6
- residual: bfloat16 [2048, 2560], P(('ep', 'dp')), may hold values from -30 to 30
- out_weight: bfloat16 [2560, 2560], P(None, 'dp'), may hold values from -0.125 to 0.125
- pre_gain: float32 [2560], replicated, may hold values from 0.5 to 1.5
- routes: int32 [2048, 6], P(('ep', 'dp')), may hold values from 0 to 15, all different within a row; in each aligned block of 64 rows (0 to 63, 64 to 127, ...) at most 36 rows name the same one
- gate_prob: float32 [2048, 6], P(('ep', 'dp')), may hold values from 0.05 to 1
- gate_weight: bfloat16 [16, 2560, 1536], P('ep', None, 'dp'), may hold values from -0.125 to 0.125
- up_weight: bfloat16 [16, 2560, 1536], P('ep', None, 'dp'), may hold values from -0.125 to 0.125
- down_weight: bfloat16 [16, 1536, 2560], P('ep', None, 'dp'), may hold values from -0.15625 to 0.15625
- post_gain: float32 [2560], replicated, may hold values from 0.5 to 1.5
Outputs:
- new_state: bfloat16 [2048, 2560], P(('ep', 'dp'))
- normed_state: bfloat16 [2048, 2560], P(('ep', 'dp'))
The draws below stay inside these ranges and needn't reach their ends.
Inputs may be any that keep to these rules, and one draw needn't show every extreme that they name: `routes`: each row names 6 different experts; within the 64 rows of one device no expert is named more than 36 times, a bound that some block reaches.
All inputs are finite; a program needn't handle non-finite values.
Results may differ from the reference program's by a relative error of at most 0.015.
Values may be sent and summed in bfloat16 or wider, within the bound.
A program may use at most 128 MiB of HBM per device.

```python
import math
import jax
import jax.numpy as jnp
import numpy as np
from jax import lax

D = 2560
FF = 1536
TOP = 6
TOK_DEV = 64
ATT = 2560
EXPERTS = 16
CAP = 36
TOKENS = 2048
N_EP = 16
N_DP = 2


def draw_residual(key, part):
    first_key, second_key = jax.random.split(key)
    scales = jnp.exp(jax.random.uniform(first_key, (TOKENS, 1), jnp.float32, math.log(0.3), math.log(3.0)))
    base = jnp.clip(jax.random.normal(second_key, (TOKENS, D), jnp.float32), -6.0, 6.0)
    return (scales * base).astype(jnp.bfloat16)


def block_levels(rng, extent, cuts, smallest, high):
    def one(axis_at, shards_of):
        draws = jax.random.uniform(jax.random.fold_in(jax.random.fold_in(rng, 6), axis_at), (shards_of,), jnp.float32, smallest / len(cuts), high / len(cuts))
        return jnp.repeat(jnp.exp(draws), extent[axis_at] // shards_of).reshape((-1,) + (1,) * (len(extent) - axis_at - 1))

    loudness = one(*cuts[0])
    for cut in cuts[1:]:
        loudness = loudness * one(*cut)
    return loudness


def shared_out(stream_key, own, number, rows, count, top, limit, skew):
    ranking = jax.random.permutation(stream_key, count)
    heavy_load, common = load_shares(count, rows * top, limit, skew, True), load_shares(count, rows * top, limit, skew, False)
    places = jnp.arange(count)

    def named(lengths, turn):
        used = int((lengths > 0).sum())
        fixed = max(1, used // 4)
        passed = fixed + (places - fixed + turn * (used - fixed)) % max(1, count - fixed)
        return jnp.zeros((count,), jnp.int32).at[ranking[jnp.where(places < fixed, places, passed)]].set(jnp.asarray(lengths, jnp.int32))

    lengths = jnp.where(number % 4 == 0, named(heavy_load, number // 4), named(common, number - number // 4 - 1))
    mixed = jax.random.permutation(jax.random.fold_in(own, 3), count)
    source_of, taker = mixed[0:count // 2 * 2:2], mixed[1:count // 2 * 2:2]
    slack = jnp.minimum(lengths[source_of] - 1, limit - lengths[taker]) // 2
    slack = jnp.where((source_of == ranking[0]) | (taker == ranking[0]) | (lengths[taker] == 0), 0, jnp.maximum(slack, 0))
    passed = jax.random.randint(jax.random.fold_in(own, 4), (count // 2,), 0, 1 << 20) % (slack + 1)
    lengths = lengths.at[source_of].add(-passed).at[taker].add(passed)
    labels = jnp.searchsorted(jnp.cumsum(lengths), jnp.arange(rows * top), side="right").astype(jnp.int32)
    grid = labels.reshape(top, rows).T
    grid = grid[jax.random.permutation(jax.random.fold_in(own, 1), rows)]
    turn = jax.random.randint(jax.random.fold_in(own, 2), (rows, 1), 0, top)
    return jnp.take_along_axis(grid, (jnp.arange(top)[None, :] + turn) % top, axis=1)


def load_shares(amount, total, limit, skew, full):
    loads = [(1 << 20) // math.isqrt(grade ** skew) + 1 for grade in range(1, amount + 1)]
    largest = limit if full else min(limit, max(-(-total // amount), total * loads[0] // sum(loads)))
    least = 1 if total - largest >= amount - 1 else 0
    holding, rest = [largest] + [least] * (amount - 1), total - largest - least * (amount - 1)
    while rest > 0:
        candidates = [i for i in range(1, amount) if holding[i] < largest] or [i for i in range(1, amount) if holding[i] < limit]
        whole, remaining = sum([loads[i] for i in candidates]), rest
        for i in candidates:
            more = min(limit - holding[i], max(1, remaining * loads[i] // whole), rest)
            holding[i] = holding[i] + more
            rest = rest - more
    return np.array(holding)


def normal_values(stream_key, extent, scale, limit, pieces=(), kind=jnp.bfloat16):
    values = jax.random.normal(stream_key, extent, jnp.float32) * scale
    if len(pieces) > 0:
        values = block_levels(stream_key, extent, pieces, -0.22, 0.18) * values
    return jnp.clip(values, min=-limit, max=limit).astype(kind)


def setup_inputs(seed: int = 0) -> dict:
    keys = jax.random.split(jax.random.key(seed), 11)
    attention_out = normal_values(keys[0], (TOKENS, ATT), 1.0, 6.0, ((0, 32),))
    residual = draw_residual(jax.random.fold_in(keys[10], 71), 0)
    out_weight = normal_values(keys[2], (ATT, D), ATT ** -0.5, 0.125, ((1, 2),))
    pre_gain = jnp.clip(1.0 + 0.1 * jax.random.normal(keys[3], (D,), jnp.float32), 0.5, 1.5)
    routes_keys = jax.random.split(jax.random.fold_in(keys[4], 1), TOKENS // TOK_DEV)
    routes_turns = jax.random.permutation(jax.random.fold_in(keys[4], 3), TOKENS // TOK_DEV)
    routes = jax.vmap(lambda own, number: shared_out(jax.random.fold_in(keys[4], 2), own, number, TOK_DEV, EXPERTS, TOP, CAP, 2))(routes_keys, routes_turns).reshape((TOKENS, TOP))
    gate_prob = jnp.clip(jnp.exp(math.log(1.0) - 2.9957323 * jax.random.uniform(keys[5], (TOKENS, TOP), jnp.float32) ** block_levels(keys[5], (TOKENS, TOP), ((0, 32),), -0.2, 0.2)), 0.05, 1.0)
    gate_weight = normal_values(keys[6], (EXPERTS, D, FF), D ** -0.5, 0.125, ((0, 16), (2, 2)))
    up_weight = normal_values(keys[7], (EXPERTS, D, FF), D ** -0.5, 0.125, ((0, 16), (2, 2)))
    down_weight = normal_values(keys[8], (EXPERTS, FF, D), FF ** -0.5, 0.15625, ((0, 16), (2, 2)))
    post_gain = jnp.clip(1.0 + 0.1 * jax.random.normal(keys[9], (D,), jnp.float32), 0.5, 1.5)
    return dict(attention_out=attention_out, residual=residual, out_weight=out_weight, pre_gain=pre_gain, routes=routes, gate_prob=gate_prob, gate_weight=gate_weight, up_weight=up_weight, down_weight=down_weight, post_gain=post_gain)


def rms_scale(values, gain):
    widened = values.astype(jnp.float32)
    meansq = lax.optimization_barrier(jnp.mean(widened * widened, axis=-1, keepdims=True))
    return widened * lax.rsqrt(meansq + 1e-06) * gain

def slot_table(route_block, experts, capacity):
    flat_ids = route_block.reshape(-1)
    onehot = (flat_ids[:, None] == jnp.arange(experts, dtype=jnp.int32)[None, :]).astype(jnp.int32)
    before = jnp.cumsum(onehot, axis=0) - onehot
    rank_in = lax.optimization_barrier(jnp.sum(before * onehot, axis=1))
    return (flat_ids * capacity + rank_in).reshape(route_block.shape)

def reference(attention_out, residual, out_weight, pre_gain, routes, gate_prob, gate_weight, up_weight, down_weight, post_gain):
    proj = jnp.dot(attention_out, out_weight, preferred_element_type=jnp.float32)
    summed = (residual.astype(jnp.float32) + proj).astype(jnp.bfloat16)
    normed_in = rms_scale(summed, pre_gain).astype(jnp.bfloat16)
    dev_count = N_EP * N_DP
    blocks = routes.reshape(dev_count, TOK_DEV, TOP)
    slot_ids = jax.vmap(lambda blk: slot_table(blk, EXPERTS, CAP))(blocks)
    expert_ids = slot_ids // CAP
    rank_in = slot_ids % CAP
    device_ids = jnp.arange(dev_count, dtype=jnp.int32)[:, None, None]
    position = (device_ids * CAP + rank_in).astype(jnp.int32)
    token_ids = device_ids * TOK_DEV + jnp.arange(TOK_DEV, dtype=jnp.int32)[None, :, None]
    token_ids = jnp.broadcast_to(token_ids, slot_ids.shape).astype(jnp.int32)
    buffer_ids = jnp.full((EXPERTS, dev_count * CAP), TOKENS, jnp.int32)
    buffer_ids = buffer_ids.at[expert_ids, position].set(token_ids)
    padded = jnp.concatenate([normed_in, jnp.zeros((1, D), jnp.bfloat16)], axis=0)

    def run_expert(index):
        rows_in = padded[buffer_ids[index]]
        gate_part = jnp.dot(rows_in, gate_weight[index], preferred_element_type=jnp.float32)
        up_part = jnp.dot(rows_in, up_weight[index], preferred_element_type=jnp.float32)
        hidden = (jax.nn.silu(gate_part) * up_part).astype(jnp.bfloat16)
        return jnp.dot(hidden, down_weight[index], preferred_element_type=jnp.float32).astype(jnp.bfloat16)
    results = lax.map(run_expert, jnp.arange(EXPERTS, dtype=jnp.int32))
    weight = gate_prob / lax.optimization_barrier(jnp.sum(gate_prob, axis=1, keepdims=True))
    picked = results[expert_ids.reshape(TOKENS, TOP), position.reshape(TOKENS, TOP)]
    expert_sum = jnp.einsum('tk,tkd->td', weight.astype(jnp.float32), picked.astype(jnp.float32), precision=lax.Precision.HIGHEST)
    new_state = (summed.astype(jnp.float32) + expert_sum).astype(jnp.bfloat16)
    normed_state = rms_scale(new_state, post_gain).astype(jnp.bfloat16)
    return (new_state, normed_state)
```

```python
import functools

import jax
import jax.numpy as jnp
from jax import lax
from jax.experimental import pallas as pl
from jax.experimental.pallas import tpu as pltpu
from jax.sharding import PartitionSpec as P


def rms_scale(values, gain):
    widened = values.astype(jnp.float32)
    meansq = jnp.mean(widened * widened, axis=-1, keepdims=True)
    return widened * lax.rsqrt(meansq + 1e-06) * gain


def slot_table(route_block, experts, capacity):
    flat_ids = route_block.reshape(-1)
    onehot = (flat_ids[:, None] == jnp.arange(experts, dtype=jnp.int32)[None, :]).astype(jnp.int32)
    order = jnp.arange(flat_ids.shape[0], dtype=jnp.int32)
    earlier = (order[None, :] < order[:, None]).astype(jnp.bfloat16)
    before = jnp.dot(
        earlier, onehot.astype(jnp.bfloat16), preferred_element_type=jnp.float32
    ).astype(jnp.int32)
    rank_in = jnp.sum(before * onehot, axis=1)
    return (flat_ids * capacity + rank_in).reshape(route_block.shape)


def routed_by_collectives(
    attention_out,
    residual,
    out_weight,
    pre_gain,
    routes,
    gate_prob,
    gate_weight,
    up_weight,
    down_weight,
    post_gain,
):
    groups = lax.axis_size("dp")
    experts = lax.axis_size("ep")
    tok_rows, top_picks = routes.shape
    row_width = residual.shape[1]
    part_cols = out_weight.shape[1]
    capacity = max(2, 3 * tok_rows * top_picks // (2 * experts))
    columns = jnp.dot(
        lax.all_gather(attention_out, "dp", axis=0, tiled=True),
        out_weight,
        preferred_element_type=jnp.float32,
    )
    home_cols = lax.all_to_all(
        columns.reshape(groups, tok_rows, part_cols).astype(jnp.bfloat16),
        "dp",
        split_axis=0,
        concat_axis=2,
        tiled=True,
    ).astype(jnp.float32)
    summed = (residual.astype(jnp.float32) + home_cols.reshape(tok_rows, row_width)).astype(
        jnp.bfloat16
    )
    normed_in = rms_scale(summed, pre_gain).astype(jnp.bfloat16)
    slot_ids = slot_table(routes, experts, capacity)
    matches = (
        slot_ids[:, :, None] == jnp.arange(experts * capacity, dtype=jnp.int32)[None, None, :]
    ).astype(jnp.float32)
    placing = jnp.sum(matches, axis=1).astype(jnp.bfloat16)
    weights = gate_prob / jnp.sum(gate_prob, axis=1, keepdims=True)
    mixing = jnp.sum(weights[:, :, None] * matches, axis=1)
    outgoing = lax.dot_general(
        placing, normed_in, (((0,), (0,)), ((), ())), preferred_element_type=jnp.float32
    ).astype(jnp.bfloat16)
    gate_local = gate_weight[0]
    up_local = up_weight[0]
    down_local = down_weight[0]
    arrived = lax.all_to_all(
        outgoing.reshape(experts, capacity, row_width),
        "ep",
        split_axis=0,
        concat_axis=0,
        tiled=True,
    )
    segment = lax.all_gather(arrived.reshape(-1, row_width), "dp", axis=0, tiled=True)
    gate_part = jnp.dot(segment, gate_local, preferred_element_type=jnp.float32)
    up_part = jnp.dot(segment, up_local, preferred_element_type=jnp.float32)
    hidden = (jax.nn.silu(gate_part) * up_part).astype(jnp.bfloat16)
    results = jnp.dot(
        lax.all_gather(hidden, "dp", axis=1, tiled=True),
        down_local,
        preferred_element_type=jnp.float32,
    ).astype(jnp.bfloat16)
    joined = lax.all_to_all(
        results.reshape(groups, experts * capacity, part_cols),
        "dp",
        split_axis=0,
        concat_axis=2,
        tiled=True,
    )
    returned_rows = lax.all_to_all(
        joined.reshape(experts, capacity, row_width), "ep", split_axis=0, concat_axis=0, tiled=True
    )
    returned = returned_rows.reshape(experts * capacity, row_width).astype(jnp.float32)
    expert_sum = jnp.dot(
        mixing, returned, precision=lax.Precision.HIGHEST, preferred_element_type=jnp.float32
    )
    new_state = (summed.astype(jnp.float32) + expert_sum).astype(jnp.bfloat16)
    normed_state = rms_scale(new_state, post_gain).astype(jnp.bfloat16)
    return (new_state, normed_state)


MESH = pl.DeviceIdType.MESH
NZ = 4
NP = 4
IN_PARTS = 5
OUT_PARTS = 5


def remote(src, dst, send, recv, device):
    return pltpu.make_async_remote_copy(
        src_ref=src,
        dst_ref=dst,
        send_sem=send,
        recv_sem=recv,
        device_id=device,
        device_id_type=MESH,
    )


def fused_kernel(
    cap,
    att,
    res,
    pre,
    post,
    picks,
    probs,
    wo_hbm,
    wg_hbm,
    wu_hbm,
    wd_hbm,
    new_ref,
    normed_ref,
    wo,
    wg,
    wu,
    wd,
    att2,
    psend,
    precv,
    halves,
    smd,
    info,
    icol,
    comb,
    place,
    mix,
    xcol,
    stage,
    xs,
    acc_g,
    acc_u,
    hid,
    yst,
    ret,
    part,
    chain,
    dn,
    up,
    fsend,
    frecv,
    wsem,
    misc_s,
    misc_r,
    info_s,
    info_r,
    z_s,
    z_r,
    p_s,
    p_r,
    f_s,
    f_r,
    h_s,
    h_r,
    y_s,
    y_r,
    dn_s,
    dn_r,
    up_s,
    up_r,
):
    f32, bf16 = jnp.float32, jnp.bfloat16
    ep, c = lax.axis_index("ep"), lax.axis_index("dp")
    z, mp = ep // NP, ep % NP
    rows, width = att.shape
    half = width // 2
    slots = NZ * cap
    kw = xcol.shape[2]
    nw = yst.shape[2]
    sib = (ep, 1 - c)

    def zdev(other):
        return (other * NP + mp, c)

    def pdev(other):
        return (z * NP + other, c)

    def multiple(v, m):
        return pl.multiple_of(v, m)

    barrier = pltpu.get_barrier_semaphore()
    pl.semaphore_signal(barrier, inc=1, device_id=sib, device_id_type=MESH)
    for k in range(1, NZ):
        pl.semaphore_signal(barrier, inc=1, device_id=zdev((z + k) % NZ), device_id_type=MESH)
    for k in range(1, NP):
        pl.semaphore_signal(barrier, inc=1, device_id=pdev((mp + k) % NP), device_id_type=MESH)
    loads = [
        pltpu.make_async_copy(wo_hbm, wo, wsem.at[0]),
        pltpu.make_async_copy(wg_hbm.at[0], wg, wsem.at[1]),
        pltpu.make_async_copy(wu_hbm.at[0], wu, wsem.at[2]),
        pltpu.make_async_copy(wd_hbm.at[0], wd, wsem.at[3]),
    ]
    for load in loads:
        load.start()
    att2[0:rows, :] = att[...]
    pl.semaphore_wait(barrier, NZ + NP - 1)
    send_att = remote(
        att2.at[pl.ds(0, rows)], att2.at[pl.ds(rows, rows)], misc_s.at[0], misc_r.at[0], sib
    )
    send_att.start()

    lanes = NZ * rows
    experts = NZ * NP
    lane = lax.broadcasted_iota(jnp.int32, (experts, lanes), 1)
    expert = lax.broadcasted_iota(jnp.int32, (experts, lanes), 0)
    mine = (lane >= z * rows) & (lane < (z + 1) * rows)
    prob = probs[...]
    weight = prob / jnp.sum(prob, axis=0, keepdims=True)
    chosen = jnp.zeros((experts, lanes), f32)
    weighted = jnp.zeros((experts, lanes), f32)
    for k in range(picks.shape[0]):
        hit = (picks[k : k + 1, :] == expert) & mine
        chosen = chosen + jnp.where(hit, 1.0, 0.0)
        weighted = weighted + jnp.where(hit, weight[k : k + 1, :], 0.0)
    earlier = (
        lax.broadcasted_iota(jnp.int32, (lanes, lanes), 0)
        < lax.broadcasted_iota(jnp.int32, (lanes, lanes), 1)
    )
    rank = jnp.dot(
        chosen.astype(bf16), jnp.where(earlier, 1.0, 0.0).astype(bf16), preferred_element_type=f32
    )
    offset = (z * cap).astype(f32)
    target = jnp.where(mine, jnp.where(chosen > 0.5, rank + offset, -1.0), 0.0)
    for k in range(NZ):
        info[k, 0:NP, :] = target[k * NP : (k + 1) * NP, :]
        info[k, NP : 2 * NP, :] = weighted[k * NP : (k + 1) * NP, :]
    info_sends = []
    for k in range(1, NZ):
        other = (z + k) % NZ
        info_sends.append(
            remote(info.at[other], icol.at[z], info_s.at[other], info_r.at[z], zdev(other))
        )
        info_sends[-1].start()
    icol[z] = info[z]
    acc_g[...] = jnp.zeros_like(acc_g)
    acc_u[...] = jnp.zeros_like(acc_u)

    loads[0].wait()
    send_att.wait_recv()

    @pl.loop(0, half // 256)
    def _(n):
        cols = pl.ds(multiple(n * 256, 256), 256)
        tile = jnp.dot(att2[...], wo[:, cols], preferred_element_type=f32)
        halves[c, :, cols] = tile[0:rows]
        psend[:, cols] = tile[rows:].astype(bf16)

    send_proj = remote(psend, precv, misc_s.at[1], misc_r.at[1], sib)
    send_proj.start()
    for k in range(1, NZ):
        other = (z + k) % NZ
        remote(
            info.at[other], icol.at[other], info_s.at[other], info_r.at[other], zdev(other)
        ).wait_recv()
    comb[c] = icol[0] + icol[1] + icol[2] + icol[3]
    send_comb = remote(comb.at[c], comb.at[c], misc_s.at[2], misc_r.at[2], sib)
    send_comb.start()
    slot = lax.broadcasted_iota(jnp.int32, (slots, lanes), 0).astype(f32)
    routed = comb[c]
    for p in range(NP):
        place[p * slots : (p + 1) * slots, :] = jnp.where(
            slot == routed[p : p + 1, :], 1.0, 0.0
        ).astype(bf16)
    send_proj.wait_recv()
    halves[1 - c] = precv[...].astype(f32)
    squares = jnp.zeros((rows, 1), f32)
    for h in range(2):
        summed = (res[:, h * half : (h + 1) * half].astype(f32) + halves[h]).astype(bf16)
        smd[:, h * half : (h + 1) * half] = summed
        wide = summed.astype(f32)
        squares = squares + jnp.sum(wide * wide, axis=1, keepdims=True)
    scale = lax.rsqrt(squares / width + 1e-06)
    own = pl.ds(multiple(z * rows, rows), rows)
    for j in range(IN_PARTS):
        cols = slice(j * kw, (j + 1) * kw)
        xcol[j, own, :] = (smd[:, cols].astype(f32) * scale * pre[:, cols]).astype(bf16)

    def zblock(j, b):
        return xcol.at[j, pl.ds(multiple(b * rows, rows), rows)]

    def zcopy(j, b, d):
        return remote(
            zblock(j, b),
            zblock(j, b),
            z_s.at[d, j, b],
            z_r.at[j, b],
            zdev(jnp.where(d == 0, z + 1, z - 1)),
        )

    def pick_copy(j, q, device):
        return remote(
            stage.at[j, pl.ds(multiple(q * slots, 16), slots)],
            xs.at[j, pl.ds(multiple(mp * 2 * slots + c * slots, 16), slots)],
            p_s.at[j, q],
            p_r.at[j, mp],
            device,
        )

    def landed(j, q, core):
        return xs.at[j, pl.ds(multiple(q * 2 * slots + core * slots, 16), slots)]

    def pass_on(j, q):
        return remote(landed(j, q, c), landed(j, q, c), f_s.at[j, q], f_r.at[j, q], sib)

    for j in range(IN_PARTS):

        @pl.when(z < NZ - 1)
        def _():
            zcopy(j, z, 0).start()

        @pl.when(z > 0)
        def _():
            zcopy(j, z, 1).start()

    loads[1].wait()
    loads[2].wait()

    @pl.loop(0, IN_PARTS + 4)
    def _(t):
        for d in range(1, NZ):
            j = t - (d - 1)
            ready = (j >= 0) & (j < IN_PARTS)

            @pl.when(ready & (z - d >= 0))
            def _():
                zcopy(j, z - d, 0).wait_recv()

                @pl.when(z < NZ - 1)
                def _():
                    zcopy(j, z - d, 0).start()

            @pl.when(ready & (z + d < NZ))
            def _():
                zcopy(j, z + d, 1).wait_recv()

                @pl.when(z > 0)
                def _():
                    zcopy(j, z + d, 1).start()

        j2 = t - 2

        @pl.when((j2 >= 0) & (j2 < IN_PARTS))
        def _():
            stage[j2] = jnp.dot(place[...], xcol[j2], preferred_element_type=f32).astype(bf16)
            for k in range(1, NP):
                q = (mp + k) % NP
                pick_copy(j2, q, pdev(q)).start()
            landed(j2, mp, c)[...] = stage[j2, pl.ds(multiple(mp * slots, 16), slots), :]
            pass_on(j2, mp).start()

        j3 = t - 3

        @pl.when((j3 >= 0) & (j3 < IN_PARTS))
        def _():
            for k in range(1, NP):
                q = (mp + k) % NP
                remote(
                    landed(j3, q, c), landed(j3, q, c), p_s.at[j3, q], p_r.at[j3, q], pdev(q)
                ).wait_recv()
                pass_on(j3, q).start()

        j4 = t - 4

        @pl.when((j4 >= 0) & (j4 < IN_PARTS))
        def _():
            for q in range(NP):
                remote(
                    landed(j4, q, 1 - c), landed(j4, q, 1 - c), f_s.at[j4, q], f_r.at[j4, q], sib
                ).wait_recv()

            @pl.loop(0, acc_g.shape[1] // 256)
            def _(n):
                cols = pl.ds(multiple(n * 256, 256), 256)
                deep = pl.ds(multiple(j4 * kw, kw), kw)
                acc_g[:, cols] += jnp.dot(xs[j4], wg[deep, cols], preferred_element_type=f32)
                acc_u[:, cols] += jnp.dot(xs[j4], wu[deep, cols], preferred_element_type=f32)

    tiles = acc_g.shape[1] // 256
    for n in range(tiles):
        cols = slice(n * 256, (n + 1) * 256)
        gate = acc_g[:, cols]
        hid[c, n] = (gate / (1.0 + jnp.exp(-gate)) * acc_u[:, cols]).astype(bf16)
        remote(hid.at[c, n], hid.at[c, n], h_s.at[n], h_r.at[n], sib).start()

    send_comb.wait_send()
    remote(comb.at[1 - c], comb.at[1 - c], misc_s.at[2], misc_r.at[2], sib).wait_recv()
    for core in range(2):
        routed = comb[core]
        for p in range(NP):
            spread = jnp.where(slot == routed[p : p + 1, :], routed[NP + p : NP + p + 1, :], 0.0)
            high = spread.astype(bf16)
            low = (spread - high.astype(f32)).astype(bf16)
            mix[core, 0, p * slots : (p + 1) * slots, :] = high
            mix[core, 1, p * slots : (p + 1) * slots, :] = low

    loads[3].wait()
    for n in range(tiles):
        remote(hid.at[1 - c, n], hid.at[1 - c, n], h_s.at[n], h_r.at[n], sib).wait_recv()

    def answer(r, q):
        return yst.at[r, pl.ds(multiple(q * 2 * slots, 16), 2 * slots)]

    def back(r, q):
        return remote(answer(r, q), ret.at[r, mp], y_s.at[r, q], y_r.at[r, mp], pdev(q))

    def dn_copy(r, b):
        return remote(chain.at[r, b], dn.at[r, b], dn_s.at[r, b], dn_r.at[r, b], zdev(z - 1))

    def up_copy(r, b):
        return remote(chain.at[r, b], up.at[r, b], up_s.at[r, b], up_r.at[r, b], zdev(z + 1))

    @pl.loop(0, OUT_PARTS + 3)
    def _(t):
        @pl.when(t < OUT_PARTS)
        def _():
            cols = pl.ds(multiple(t * nw, nw), nw)
            total = jnp.zeros((yst.shape[1], nw), f32)
            for h in range(2):
                for n in range(tiles):
                    first = (h * tiles + n) * 256
                    total = total + jnp.dot(
                        hid[h, n], wd[first : first + 256, cols], preferred_element_type=f32
                    )
            yst[t] = total.astype(bf16)
            for k in range(1, NP):
                q = (mp + k) % NP
                back(t, q).start()
            ret[t, mp] = yst[t, pl.ds(multiple(mp * 2 * slots, 16), 2 * slots), :]

        r1 = t - 1

        @pl.when((r1 >= 0) & (r1 < OUT_PARTS))
        def _():
            for k in range(1, NP):
                q = (mp + k) % NP
                remote(
                    answer(r1, q), ret.at[r1, q], y_s.at[r1, q], y_r.at[r1, q], pdev(q)
                ).wait_recv()
            for core in range(2):
                total = jnp.zeros((lanes, nw), f32)
                for p in range(NP):
                    got = ret[r1, p, core * slots : (core + 1) * slots, :]
                    for term in range(2):
                        total = total + lax.dot_general(
                            mix[core, term, p * slots : (p + 1) * slots, :],
                            got,
                            (((0,), (0,)), ((), ())),
                            preferred_element_type=f32,
                        )
                for b in range(NZ):
                    part[r1, b, core * rows : (core + 1) * rows, :] = total[
                        b * rows : (b + 1) * rows
                    ]

        rd = t - 1 - (NZ - 1 - z)

        @pl.when((rd >= 0) & (rd < OUT_PARTS))
        def _():
            for b in range(NZ - 1):

                @pl.when((b < z) & (z == NZ - 1))
                def _():
                    chain[rd, b] = part[rd, b].astype(bf16)
                    dn_copy(rd, b).start()

                @pl.when((b < z) & (z < NZ - 1))
                def _():
                    dn_copy(rd, b).wait_recv()
                    chain[rd, b] = (part[rd, b] + dn[rd, b].astype(f32)).astype(bf16)
                    dn_copy(rd, b).start()

        ru = t - 1 - z

        @pl.when((ru >= 0) & (ru < OUT_PARTS))
        def _():
            for b in range(1, NZ):

                @pl.when((b > z) & (z == 0))
                def _():
                    chain[ru, b] = part[ru, b].astype(bf16)
                    up_copy(ru, b).start()

                @pl.when((b > z) & (z > 0))
                def _():
                    up_copy(ru, b).wait_recv()
                    chain[ru, b] = (part[ru, b] + up[ru, b].astype(f32)).astype(bf16)
                    up_copy(ru, b).start()

    for r in range(OUT_PARTS):
        cols = slice(r * nw, (r + 1) * nw)

        @pl.when(z < NZ - 1)
        def _():
            dn_copy(r, z).wait_recv()
            part[r, z] = part[r, z] + dn[r, z].astype(f32)

        @pl.when(z > 0)
        def _():
            up_copy(r, z).wait_recv()
            part[r, z] = part[r, z] + up[r, z].astype(f32)

        halves[c, :, cols] = part[r, z, pl.ds(multiple(c * rows, rows), rows), :]
        fsend[:, cols] = part[r, z, pl.ds(multiple((1 - c) * rows, rows), rows), :]
    send_last = remote(fsend, frecv, misc_s.at[3], misc_r.at[3], sib)
    send_last.start()
    send_last.wait_recv()
    halves[1 - c] = frecv[...]
    squares = jnp.zeros((rows, 1), f32)
    for h in range(2):
        cols = slice(h * half, (h + 1) * half)
        state = (smd[:, cols].astype(f32) + halves[h]).astype(bf16)
        new_ref[:, cols] = state
        wide = state.astype(f32)
        squares = squares + jnp.sum(wide * wide, axis=1, keepdims=True)
    scale = lax.rsqrt(squares / width + 1e-06)
    for h in range(2):
        cols = slice(h * half, (h + 1) * half)
        normed_ref[:, cols] = (new_ref[:, cols].astype(f32) * scale * post[:, cols]).astype(bf16)

    send_att.wait_send()
    send_proj.wait_send()
    send_last.wait_send()
    for copy in info_sends:
        copy.wait_send()
    for n in range(tiles):
        remote(hid.at[c, n], hid.at[c, n], h_s.at[n], h_r.at[n], sib).wait_send()

    @pl.loop(0, IN_PARTS)
    def _(j):
        for b in range(NZ):

            @pl.when((z < NZ - 1) & (b <= z))
            def _():
                zcopy(j, b, 0).wait_send()

            @pl.when((z > 0) & (b >= z))
            def _():
                zcopy(j, b, 1).wait_send()

        for k in range(1, NP):
            q = (mp + k) % NP
            pick_copy(j, q, pdev(q)).wait_send()
        for q in range(NP):
            pass_on(j, q).wait_send()

    @pl.loop(0, OUT_PARTS)
    def _(r):
        for k in range(1, NP):
            q = (mp + k) % NP
            back(r, q).wait_send()
        for b in range(NZ):

            @pl.when(b < z)
            def _():
                dn_copy(r, b).wait_send()

            @pl.when(b > z)
            def _():
                up_copy(r, b).wait_send()


def fused(
    attention_out,
    residual,
    out_weight,
    pre_gain,
    routes,
    gate_prob,
    gate_weight,
    up_weight,
    down_weight,
    post_gain,
):
    rows, width = residual.shape
    top = routes.shape[1]
    half = width // 2
    hidden = gate_weight.shape[2]
    cap = max(2, 3 * rows * top // (2 * NZ * NP))
    slots = NZ * cap
    lanes = NZ * rows
    total = 2 * NP * slots
    kw, nw = width // IN_PARTS, half // OUT_PARTS
    f32, bf16 = jnp.float32, jnp.bfloat16
    dma = pltpu.SemaphoreType.DMA
    vmem = pl.BlockSpec(memory_space=pltpu.VMEM)
    hbm = pl.BlockSpec(memory_space=pl.ANY)
    return pl.pallas_call(
        functools.partial(fused_kernel, cap),
        out_shape=(
            jax.ShapeDtypeStruct((rows, width), bf16),
            jax.ShapeDtypeStruct((rows, width), bf16),
        ),
        in_specs=[vmem] * 6 + [hbm] * 4,
        out_specs=(vmem, vmem),
        scratch_shapes=[
            pltpu.VMEM((width, half), bf16),
            pltpu.VMEM((width, hidden), bf16),
            pltpu.VMEM((width, hidden), bf16),
            pltpu.VMEM((2 * hidden, half), bf16),
            pltpu.VMEM((2 * rows, width), bf16),
            pltpu.VMEM((rows, half), bf16),
            pltpu.VMEM((rows, half), bf16),
            pltpu.VMEM((2, rows, half), f32),
            pltpu.VMEM((rows, width), bf16),
            pltpu.VMEM((NZ, 2 * NP, lanes), f32),
            pltpu.VMEM((NZ, 2 * NP, lanes), f32),
            pltpu.VMEM((2, 2 * NP, lanes), f32),
            pltpu.VMEM((NP * slots, lanes), bf16),
            pltpu.VMEM((2, 2, NP * slots, lanes), bf16),
            pltpu.VMEM((IN_PARTS, lanes, kw), bf16),
            pltpu.VMEM((IN_PARTS, NP * slots, kw), bf16),
            pltpu.VMEM((IN_PARTS, total, kw), bf16),
            pltpu.VMEM((total, hidden), f32),
            pltpu.VMEM((total, hidden), f32),
            pltpu.VMEM((2, hidden // 256, total, 256), bf16),
            pltpu.VMEM((OUT_PARTS, total, nw), bf16),
            pltpu.VMEM((OUT_PARTS, NP, 2 * slots, nw), bf16),
            pltpu.VMEM((OUT_PARTS, NZ, 2 * rows, nw), f32),
            pltpu.VMEM((OUT_PARTS, NZ, 2 * rows, nw), bf16),
            pltpu.VMEM((OUT_PARTS, NZ, 2 * rows, nw), bf16),
            pltpu.VMEM((OUT_PARTS, NZ, 2 * rows, nw), bf16),
            pltpu.VMEM((rows, half), f32),
            pltpu.VMEM((rows, half), f32),
            dma((4,)),
            dma((4,)),
            dma((4,)),
            dma((NZ,)),
            dma((NZ,)),
            dma((2, IN_PARTS, NZ)),
            dma((IN_PARTS, NZ)),
            dma((IN_PARTS, NP)),
            dma((IN_PARTS, NP)),
            dma((IN_PARTS, NP)),
            dma((IN_PARTS, NP)),
            dma((hidden // 256,)),
            dma((hidden // 256,)),
            dma((OUT_PARTS, NP)),
            dma((OUT_PARTS, NP)),
            dma((OUT_PARTS, NZ)),
            dma((OUT_PARTS, NZ)),
            dma((OUT_PARTS, NZ)),
            dma((OUT_PARTS, NZ)),
        ],
        compiler_params=pltpu.CompilerParams(
            collective_id=0, has_side_effects=True, vmem_limit_bytes=62 * 1024 * 1024
        ),
    )(
        attention_out,
        residual,
        pre_gain.reshape(1, width),
        post_gain.reshape(1, width),
        jnp.tile(routes.T, (1, NZ)),
        jnp.tile(gate_prob.T, (1, NZ)),
        out_weight,
        gate_weight,
        up_weight,
        down_weight,
    )


def per_device(chips, *arrays):
    if chips == NZ * NP:
        return fused(*arrays)
    return routed_by_collectives(*arrays)


def solution(mesh):
    return jax.shard_map(
        functools.partial(per_device, mesh.shape["ep"]),
        mesh=mesh,
        in_specs=(
            P(("ep", "dp"), None),
            P(("ep", "dp"), None),
            P(None, "dp"),
            P(),
            P(("ep", "dp"), None),
            P(("ep", "dp"), None),
            P("ep", None, "dp"),
            P("ep", None, "dp"),
            P("ep", None, "dp"),
            P(),
        ),
        out_specs=(P(("ep", "dp"), None), P(("ep", "dp"), None)),
        check_vma=False,
    )
```

```python
import functools

import jax
import jax.numpy as jnp
from jax import lax
from jax.experimental import pallas as pl
from jax.experimental.pallas import tpu as pltpu
from jax.sharding import PartitionSpec as P


def rms_scale(values, gain):
    widened = values.astype(jnp.float32)
    meansq = jnp.mean(widened * widened, axis=-1, keepdims=True)
    return widened * lax.rsqrt(meansq + 1e-06) * gain


def slot_table(route_block, experts, capacity):
    flat_ids = route_block.reshape(-1)
    onehot = (flat_ids[:, None] == jnp.arange(experts, dtype=jnp.int32)[None, :]).astype(jnp.int32)
    order = jnp.arange(flat_ids.shape[0], dtype=jnp.int32)
    earlier = (order[None, :] < order[:, None]).astype(jnp.bfloat16)
    before = jnp.dot(
        earlier, onehot.astype(jnp.bfloat16), preferred_element_type=jnp.float32
    ).astype(jnp.int32)
    rank_in = jnp.sum(before * onehot, axis=1)
    return (flat_ids * capacity + rank_in).reshape(route_block.shape)


def routed_by_collectives(
    attention_out,
    residual,
    out_weight,
    pre_gain,
    routes,
    gate_prob,
    gate_weight,
    up_weight,
    down_weight,
    post_gain,
):
    groups = lax.axis_size("dp")
    experts = lax.axis_size("ep")
    tok_rows, top_picks = routes.shape
    row_width = residual.shape[1]
    part_cols = out_weight.shape[1]
    capacity = max(2, 3 * tok_rows * top_picks // (2 * experts))
    columns = jnp.dot(
        lax.all_gather(attention_out, "dp", axis=0, tiled=True),
        out_weight,
        preferred_element_type=jnp.float32,
    )
    home_cols = lax.all_to_all(
        columns.reshape(groups, tok_rows, part_cols).astype(jnp.bfloat16),
        "dp",
        split_axis=0,
        concat_axis=2,
        tiled=True,
    ).astype(jnp.float32)
    summed = (residual.astype(jnp.float32) + home_cols.reshape(tok_rows, row_width)).astype(
        jnp.bfloat16
    )
    normed_in = rms_scale(summed, pre_gain).astype(jnp.bfloat16)
    slot_ids = slot_table(routes, experts, capacity)
    matches = (
        slot_ids[:, :, None] == jnp.arange(experts * capacity, dtype=jnp.int32)[None, None, :]
    ).astype(jnp.float32)
    placing = jnp.sum(matches, axis=1).astype(jnp.bfloat16)
    weights = gate_prob / jnp.sum(gate_prob, axis=1, keepdims=True)
    mixing = jnp.sum(weights[:, :, None] * matches, axis=1)
    outgoing = lax.dot_general(
        placing, normed_in, (((0,), (0,)), ((), ())), preferred_element_type=jnp.float32
    ).astype(jnp.bfloat16)
    gate_local = gate_weight[0]
    up_local = up_weight[0]
    down_local = down_weight[0]
    arrived = lax.all_to_all(
        outgoing.reshape(experts, capacity, row_width),
        "ep",
        split_axis=0,
        concat_axis=0,
        tiled=True,
    )
    segment = lax.all_gather(arrived.reshape(-1, row_width), "dp", axis=0, tiled=True)
    gate_part = jnp.dot(segment, gate_local, preferred_element_type=jnp.float32)
    up_part = jnp.dot(segment, up_local, preferred_element_type=jnp.float32)
    hidden = (jax.nn.silu(gate_part) * up_part).astype(jnp.bfloat16)
    results = jnp.dot(
        lax.all_gather(hidden, "dp", axis=1, tiled=True),
        down_local,
        preferred_element_type=jnp.float32,
    ).astype(jnp.bfloat16)
    joined = lax.all_to_all(
        results.reshape(groups, experts * capacity, part_cols),
        "dp",
        split_axis=0,
        concat_axis=2,
        tiled=True,
    )
    returned_rows = lax.all_to_all(
        joined.reshape(experts, capacity, row_width), "ep", split_axis=0, concat_axis=0, tiled=True
    )
    returned = returned_rows.reshape(experts * capacity, row_width).astype(jnp.float32)
    expert_sum = jnp.dot(
        mixing, returned, precision=lax.Precision.HIGHEST, preferred_element_type=jnp.float32
    )
    new_state = (summed.astype(jnp.float32) + expert_sum).astype(jnp.bfloat16)
    normed_state = rms_scale(new_state, post_gain).astype(jnp.bfloat16)
    return (new_state, normed_state)


MESH = pl.DeviceIdType.MESH
NZ = 4
NP = 4
IN_PARTS = 5
AHEAD = 2
OUT_PARTS = 5


def remote(src, dst, send, recv, device):
    return pltpu.make_async_remote_copy(
        src_ref=src,
        dst_ref=dst,
        send_sem=send,
        recv_sem=recv,
        device_id=device,
        device_id_type=MESH,
    )


def fused_kernel(
    cap,
    att_hbm,
    res_hbm,
    pre_hbm,
    picks_hbm,
    probs_hbm,
    wo_hbm,
    wg_hbm,
    wu_hbm,
    wd_hbm,
    sum_ref,
    expert_ref,
    res,
    pre,
    picks,
    probs,
    wo,
    wg,
    wu,
    wd,
    att2,
    psend,
    precv,
    halves,
    smd,
    info,
    icol,
    comb,
    place,
    mix,
    xcol,
    stage,
    xs,
    acc_g,
    acc_u,
    hid,
    yst,
    ret,
    part,
    chain,
    dn,
    up,
    fsend,
    frecv,
    wsem,
    misc_s,
    misc_r,
    info_s,
    info_r,
    z_s,
    z_r,
    p_s,
    p_r,
    f_s,
    f_r,
    h_s,
    h_r,
    y_s,
    y_r,
    dn_s,
    dn_r,
    up_s,
    up_r,
    proj_s,
    proj_r,
    last_s,
    last_r,
):
    f32, bf16 = jnp.float32, jnp.bfloat16
    ep, c = lax.axis_index("ep"), lax.axis_index("dp")
    z, mp = ep // NP, ep % NP
    rows, width = res.shape
    half = width // 2
    slots = NZ * cap
    kw = xcol.shape[2]
    nw = yst.shape[2]
    sib = (ep, 1 - c)

    def zdev(other):
        return (other * NP + mp, c)

    def pdev(other):
        return (z * NP + other, c)

    def multiple(v, m):
        return pl.multiple_of(v, m)

    barrier = pltpu.get_barrier_semaphore()
    pl.semaphore_signal(barrier, inc=1, device_id=sib, device_id_type=MESH)
    for k in range(1, NZ):
        pl.semaphore_signal(barrier, inc=1, device_id=zdev((z + k) % NZ), device_id_type=MESH)
    for k in range(1, NP):
        pl.semaphore_signal(barrier, inc=1, device_id=pdev((mp + k) % NP), device_id_type=MESH)
    loads = [
        pltpu.make_async_copy(wo_hbm, wo, wsem.at[0]),
        pltpu.make_async_copy(wg_hbm.at[0], wg, wsem.at[1]),
        pltpu.make_async_copy(wu_hbm.at[0], wu, wsem.at[2]),
        pltpu.make_async_copy(wd_hbm.at[0], wd, wsem.at[3]),
    ]
    small = [
        pltpu.make_async_copy(att_hbm, att2.at[pl.ds(0, rows)], wsem.at[4]),
        pltpu.make_async_copy(picks_hbm, picks, wsem.at[5]),
        pltpu.make_async_copy(probs_hbm, probs, wsem.at[6]),
        pltpu.make_async_copy(res_hbm, res, wsem.at[7]),
        pltpu.make_async_copy(pre_hbm, pre.at[0], wsem.at[8]),
    ]
    for load in small[0:3] + loads[0:1] + small[3:]:
        load.start()
    small[0].wait()
    pl.semaphore_wait(barrier, NZ + NP - 1)
    send_att = remote(
        att2.at[pl.ds(0, rows)], att2.at[pl.ds(rows, rows)], misc_s.at[0], misc_r.at[0], sib
    )
    send_att.start()

    lanes = NZ * rows
    experts = NZ * NP
    lane = lax.broadcasted_iota(jnp.int32, (experts, lanes), 1)
    expert = lax.broadcasted_iota(jnp.int32, (experts, lanes), 0)
    mine = (lane >= z * rows) & (lane < (z + 1) * rows)
    small[1].wait()
    small[2].wait()
    spot = jnp.where(
        lax.broadcasted_iota(jnp.int32, (rows, lanes), 0) + z * rows
        == lax.broadcasted_iota(jnp.int32, (rows, lanes), 1),
        1.0,
        0.0,
    ).astype(bf16)

    def spread_out(values):
        return jnp.dot(values.astype(bf16), spot, preferred_element_type=f32)

    named = spread_out(picks[...].astype(f32)).astype(jnp.int32)
    prob = probs[...]
    share = prob / jnp.sum(prob, axis=0, keepdims=True)
    term1 = share.astype(bf16).astype(f32)
    term2 = (share - term1).astype(bf16).astype(f32)
    weight = spread_out(term1) + spread_out(term2) + spread_out(share - term1 - term2)
    chosen = jnp.zeros((experts, lanes), f32)
    weighted = jnp.zeros((experts, lanes), f32)
    for k in range(picks.shape[0]):
        hit = (named[k : k + 1, :] == expert) & mine
        chosen = chosen + jnp.where(hit, 1.0, 0.0)
        weighted = weighted + jnp.where(hit, weight[k : k + 1, :], 0.0)
    earlier = (
        lax.broadcasted_iota(jnp.int32, (lanes, lanes), 0)
        < lax.broadcasted_iota(jnp.int32, (lanes, lanes), 1)
    )
    rank = jnp.dot(
        chosen.astype(bf16), jnp.where(earlier, 1.0, 0.0).astype(bf16), preferred_element_type=f32
    )
    offset = (z * cap).astype(f32)
    target = jnp.where(mine, jnp.where(chosen > 0.5, rank + offset, -1.0), 0.0)
    for k in range(NZ):
        info[k, 0:NP, :] = target[k * NP : (k + 1) * NP, :]
        info[k, NP : 2 * NP, :] = weighted[k * NP : (k + 1) * NP, :]
    info_sends = []
    for k in range(1, NZ):
        other = (z + k) % NZ
        info_sends.append(
            remote(info.at[other], icol.at[z], info_s.at[other], info_r.at[z], zdev(other))
        )
        info_sends[-1].start()
    icol[z] = info[z]

    loads[0].wait()
    for load in loads[1:]:
        load.start()
    send_att.wait_recv()

    send_proj = []
    for n in range(half // 256):
        cols = slice(n * 256, (n + 1) * 256)
        tile = jnp.dot(att2[...], wo[:, cols], preferred_element_type=f32)
        halves[c, :, cols] = tile[0:rows]
        psend[n] = tile[rows:].astype(bf16)
        send_proj.append(remote(psend.at[n], precv.at[n], proj_s.at[n], proj_r.at[n], sib))
        send_proj[n].start()
    for k in range(1, NZ):
        other = (z + k) % NZ
        remote(
            info.at[other], icol.at[other], info_s.at[other], info_r.at[other], zdev(other)
        ).wait_recv()
    comb[c] = icol[0] + icol[1] + icol[2] + icol[3]
    send_comb = remote(comb.at[c], comb.at[c], misc_s.at[2], misc_r.at[2], sib)
    send_comb.start()
    slot = lax.broadcasted_iota(jnp.int32, (slots, lanes), 0).astype(f32)
    routed = comb[c]
    for p in range(NP):
        place[p * slots : (p + 1) * slots, :] = jnp.where(
            slot == routed[p : p + 1, :], 1.0, 0.0
        ).astype(bf16)
    for load in small[3:]:
        load.wait()
    for n in range(half // 256):
        send_proj[n].wait_recv()
        halves[1 - c, :, n * 256 : (n + 1) * 256] = precv[n].astype(f32)
    squares = jnp.zeros((rows, 1), f32)
    for h in range(2):
        summed = (res[:, h * half : (h + 1) * half].astype(f32) + halves[h]).astype(bf16)
        smd[:, h * half : (h + 1) * half] = summed
        wide = summed.astype(f32)
        squares = squares + jnp.sum(wide * wide, axis=1, keepdims=True)
    scale = lax.rsqrt(squares / width + 1e-06)
    own = pl.ds(multiple(z * rows, rows), rows)

    def zblock(j, b):
        return xcol.at[j, pl.ds(multiple(b * rows, rows), rows)]

    def zcopy(j, b, d):
        return remote(
            zblock(j, b),
            zblock(j, b),
            z_s.at[d, j, b],
            z_r.at[j, b],
            zdev(jnp.where(d == 0, z + 1, z - 1)),
        )

    def pick_copy(j, q, device):
        return remote(
            stage.at[j, pl.ds(multiple(q * slots, 16), slots)],
            xs.at[j, pl.ds(multiple(mp * 2 * slots + c * slots, 16), slots)],
            p_s.at[j, q],
            p_r.at[j, mp],
            device,
        )

    def landed(j, q, core):
        return xs.at[j, pl.ds(multiple(q * 2 * slots + core * slots, 16), slots)]

    def pass_on(j, q):
        return remote(landed(j, q, c), landed(j, q, c), f_s.at[j, q], f_r.at[j, q], sib)

    def send_own(j):
        @pl.when(z < NZ - 1)
        def _():
            zcopy(j, z, 0).start()

        @pl.when(z > 0)
        def _():
            zcopy(j, z, 1).start()

    for j in range(IN_PARTS):
        cols = slice(j * kw, (j + 1) * kw)
        xcol[j, own, :] = (smd[:, cols].astype(f32) * scale * pre[:, cols]).astype(bf16)
        if j < AHEAD:
            send_own(j)
    acc_g[...] = jnp.zeros_like(acc_g)
    acc_u[...] = jnp.zeros_like(acc_u)
    loads[1].wait()
    loads[2].wait()

    @pl.loop(0, IN_PARTS + 4)
    def _(t):
        for d in range(1, NZ):
            j = t - (d - 1)
            ready = (j >= 0) & (j < IN_PARTS)

            @pl.when(ready & (z - d >= 0))
            def _():
                zcopy(j, z - d, 0).wait_recv()

                @pl.when(z < NZ - 1)
                def _():
                    zcopy(j, z - d, 0).start()

            @pl.when(ready & (z + d < NZ))
            def _():
                zcopy(j, z + d, 1).wait_recv()

                @pl.when(z > 0)
                def _():
                    zcopy(j, z + d, 1).start()

        @pl.when(t + AHEAD < IN_PARTS)
        def _():
            send_own(t + AHEAD)

        j2 = t - 2

        @pl.when((j2 >= 0) & (j2 < IN_PARTS))
        def _():
            stage[j2] = jnp.dot(place[...], xcol[j2], preferred_element_type=f32).astype(bf16)
            for k in range(1, NP):
                q = (mp + k) % NP
                pick_copy(j2, q, pdev(q)).start()
            landed(j2, mp, c)[...] = stage[j2, pl.ds(multiple(mp * slots, 16), slots), :]
            pass_on(j2, mp).start()

        j3 = t - 3

        @pl.when((j3 >= 0) & (j3 < IN_PARTS))
        def _():
            for k in range(1, NP):
                q = (mp + k) % NP
                remote(
                    landed(j3, q, c), landed(j3, q, c), p_s.at[j3, q], p_r.at[j3, q], pdev(q)
                ).wait_recv()
                pass_on(j3, q).start()

        j4 = t - 4

        @pl.when((j4 >= 0) & (j4 < IN_PARTS))
        def _():
            for q in range(NP):
                remote(
                    landed(j4, q, 1 - c), landed(j4, q, 1 - c), f_s.at[j4, q], f_r.at[j4, q], sib
                ).wait_recv()

            @pl.loop(0, acc_g.shape[1] // 256)
            def _(n):
                cols = pl.ds(multiple(n * 256, 256), 256)
                deep = pl.ds(multiple(j4 * kw, kw), kw)
                acc_g[:, cols] += jnp.dot(xs[j4], wg[deep, cols], preferred_element_type=f32)
                acc_u[:, cols] += jnp.dot(xs[j4], wu[deep, cols], preferred_element_type=f32)

    tiles = acc_g.shape[1] // 256
    for n in range(tiles):
        cols = slice(n * 256, (n + 1) * 256)
        gate = acc_g[:, cols]
        hid[c, n] = (gate / (1.0 + jnp.exp(-gate)) * acc_u[:, cols]).astype(bf16)
        remote(hid.at[c, n], hid.at[c, n], h_s.at[n], h_r.at[n], sib).start()

    send_comb.wait_send()
    remote(comb.at[1 - c], comb.at[1 - c], misc_s.at[2], misc_r.at[2], sib).wait_recv()
    for core in range(2):
        routed = comb[core]
        for p in range(NP):
            spread = jnp.where(slot == routed[p : p + 1, :], routed[NP + p : NP + p + 1, :], 0.0)
            high = spread.astype(bf16)
            low = (spread - high.astype(f32)).astype(bf16)
            mix[core, 0, p * slots : (p + 1) * slots, :] = high
            mix[core, 1, p * slots : (p + 1) * slots, :] = low

    loads[3].wait()
    for n in range(tiles):
        remote(hid.at[1 - c, n], hid.at[1 - c, n], h_s.at[n], h_r.at[n], sib).wait_recv()

    def answer(r, q):
        return yst.at[r, pl.ds(multiple(q * 2 * slots, 16), 2 * slots)]

    def back(r, q):
        return remote(answer(r, q), ret.at[r, mp], y_s.at[r, q], y_r.at[r, mp], pdev(q))

    def dn_copy(r, b):
        return remote(chain.at[r, b], dn.at[r, b], dn_s.at[r, b], dn_r.at[r, b], zdev(z - 1))

    def up_copy(r, b):
        return remote(chain.at[r, b], up.at[r, b], up_s.at[r, b], up_r.at[r, b], zdev(z + 1))

    send_last = []

    @pl.loop(0, OUT_PARTS + 3)
    def _(t):
        @pl.when(t < OUT_PARTS)
        def _():
            cols = pl.ds(multiple(t * nw, nw), nw)
            total = jnp.zeros((yst.shape[1], nw), f32)
            for h in range(2):
                for n in range(tiles):
                    first = (h * tiles + n) * 256
                    total = total + jnp.dot(
                        hid[h, n], wd[first : first + 256, cols], preferred_element_type=f32
                    )
            yst[t] = total.astype(bf16)
            for k in range(1, NP):
                q = (mp + k) % NP
                back(t, q).start()
            ret[t, mp] = yst[t, pl.ds(multiple(mp * 2 * slots, 16), 2 * slots), :]

        r1 = t - 1

        @pl.when((r1 >= 0) & (r1 < OUT_PARTS))
        def _():
            for k in range(1, NP):
                q = (mp + k) % NP
                remote(
                    answer(r1, q), ret.at[r1, q], y_s.at[r1, q], y_r.at[r1, q], pdev(q)
                ).wait_recv()
            for core in range(2):
                total = jnp.zeros((lanes, nw), f32)
                for p in range(NP):
                    got = ret[r1, p, core * slots : (core + 1) * slots, :]
                    for term in range(2):
                        total = total + lax.dot_general(
                            mix[core, term, p * slots : (p + 1) * slots, :],
                            got,
                            (((0,), (0,)), ((), ())),
                            preferred_element_type=f32,
                        )
                for b in range(NZ):
                    part[r1, b, core * rows : (core + 1) * rows, :] = total[
                        b * rows : (b + 1) * rows
                    ]

        rd = t - 1 - (NZ - 1 - z)

        @pl.when((rd >= 0) & (rd < OUT_PARTS))
        def _():
            for b in range(NZ - 1):

                @pl.when((b < z) & (z == NZ - 1))
                def _():
                    chain[rd, b] = part[rd, b].astype(bf16)
                    dn_copy(rd, b).start()

                @pl.when((b < z) & (z < NZ - 1))
                def _():
                    dn_copy(rd, b).wait_recv()
                    chain[rd, b] = (part[rd, b] + dn[rd, b].astype(f32)).astype(bf16)
                    dn_copy(rd, b).start()

        ru = t - 1 - z

        @pl.when((ru >= 0) & (ru < OUT_PARTS))
        def _():
            for b in range(1, NZ):

                @pl.when((b > z) & (z == 0))
                def _():
                    chain[ru, b] = part[ru, b].astype(bf16)
                    up_copy(ru, b).start()

                @pl.when((b > z) & (z > 0))
                def _():
                    up_copy(ru, b).wait_recv()
                    chain[ru, b] = (part[ru, b] + up[ru, b].astype(f32)).astype(bf16)
                    up_copy(ru, b).start()

    for r in range(OUT_PARTS):
        cols = slice(r * nw, (r + 1) * nw)

        @pl.when(z < NZ - 1)
        def _():
            dn_copy(r, z).wait_recv()
            part[r, z] = part[r, z] + dn[r, z].astype(f32)

        @pl.when(z > 0)
        def _():
            up_copy(r, z).wait_recv()
            part[r, z] = part[r, z] + up[r, z].astype(f32)

        halves[c, :, cols] = part[r, z, pl.ds(multiple(c * rows, rows), rows), :]
        fsend[r] = part[r, z, pl.ds(multiple((1 - c) * rows, rows), rows), :]
        send_last.append(remote(fsend.at[r], frecv.at[r], last_s.at[r], last_r.at[r], sib))
        send_last[r].start()
    for r in range(OUT_PARTS):
        send_last[r].wait_recv()
        halves[1 - c, :, r * nw : (r + 1) * nw] = frecv[r]
    sum_ref[...] = smd[...]
    expert_ref[...] = halves[...]

    send_att.wait_send()
    for copy in send_proj + send_last:
        copy.wait_send()
    for copy in info_sends:
        copy.wait_send()
    for n in range(tiles):
        remote(hid.at[c, n], hid.at[c, n], h_s.at[n], h_r.at[n], sib).wait_send()

    @pl.loop(0, IN_PARTS)
    def _(j):
        for b in range(NZ):

            @pl.when((z < NZ - 1) & (b <= z))
            def _():
                zcopy(j, b, 0).wait_send()

            @pl.when((z > 0) & (b >= z))
            def _():
                zcopy(j, b, 1).wait_send()

        for k in range(1, NP):
            q = (mp + k) % NP
            pick_copy(j, q, pdev(q)).wait_send()
        for q in range(NP):
            pass_on(j, q).wait_send()

    @pl.loop(0, OUT_PARTS)
    def _(r):
        for k in range(1, NP):
            q = (mp + k) % NP
            back(r, q).wait_send()
        for b in range(NZ):

            @pl.when(b < z)
            def _():
                dn_copy(r, b).wait_send()

            @pl.when(b > z)
            def _():
                up_copy(r, b).wait_send()


def end_kernel(sum_ref, expert_ref, post_hbm, new_ref, normed_ref, post, sem):
    f32, bf16 = jnp.float32, jnp.bfloat16
    load = pltpu.make_async_copy(post_hbm, post.at[0], sem)
    load.start()
    rows, width = sum_ref.shape
    half = width // 2
    squares = jnp.zeros((rows, 1), f32)
    for h in range(2):
        cols = slice(h * half, (h + 1) * half)
        state = (sum_ref[:, cols].astype(f32) + expert_ref[h]).astype(bf16)
        new_ref[:, cols] = state
        wide = state.astype(f32)
        squares = squares + jnp.sum(wide * wide, axis=1, keepdims=True)
    scale = lax.rsqrt(squares / width + 1e-06)
    load.wait()
    for h in range(2):
        cols = slice(h * half, (h + 1) * half)
        normed_ref[:, cols] = (new_ref[:, cols].astype(f32) * scale * post[:, cols]).astype(bf16)


def fused(
    attention_out,
    residual,
    out_weight,
    pre_gain,
    routes,
    gate_prob,
    gate_weight,
    up_weight,
    down_weight,
    post_gain,
):
    rows, width = residual.shape
    top = routes.shape[1]
    half = width // 2
    hidden = gate_weight.shape[2]
    cap = max(2, 3 * rows * top // (2 * NZ * NP))
    slots = NZ * cap
    lanes = NZ * rows
    total = 2 * NP * slots
    kw, nw = width // IN_PARTS, half // OUT_PARTS
    f32, bf16 = jnp.float32, jnp.bfloat16
    dma = pltpu.SemaphoreType.DMA
    vmem = pl.BlockSpec(memory_space=pltpu.VMEM)
    hbm = pl.BlockSpec(memory_space=pl.ANY)
    summed, expert_sum = pl.pallas_call(
        functools.partial(fused_kernel, cap),
        out_shape=(
            jax.ShapeDtypeStruct((rows, width), bf16),
            jax.ShapeDtypeStruct((2, rows, half), f32),
        ),
        in_specs=[hbm] * 9,
        out_specs=(vmem, vmem),
        scratch_shapes=[
            pltpu.VMEM((rows, width), bf16),
            pltpu.VMEM((1, width), f32),
            pltpu.VMEM((top, rows), jnp.int32),
            pltpu.VMEM((top, rows), f32),
            pltpu.VMEM((width, half), bf16),
            pltpu.VMEM((width, hidden), bf16),
            pltpu.VMEM((width, hidden), bf16),
            pltpu.VMEM((2 * hidden, half), bf16),
            pltpu.VMEM((2 * rows, width), bf16),
            pltpu.VMEM((half // 256, rows, 256), bf16),
            pltpu.VMEM((half // 256, rows, 256), bf16),
            pltpu.VMEM((2, rows, half), f32),
            pltpu.VMEM((rows, width), bf16),
            pltpu.VMEM((NZ, 2 * NP, lanes), f32),
            pltpu.VMEM((NZ, 2 * NP, lanes), f32),
            pltpu.VMEM((2, 2 * NP, lanes), f32),
            pltpu.VMEM((NP * slots, lanes), bf16),
            pltpu.VMEM((2, 2, NP * slots, lanes), bf16),
            pltpu.VMEM((IN_PARTS, lanes, kw), bf16),
            pltpu.VMEM((IN_PARTS, NP * slots, kw), bf16),
            pltpu.VMEM((IN_PARTS, total, kw), bf16),
            pltpu.VMEM((total, hidden), f32),
            pltpu.VMEM((total, hidden), f32),
            pltpu.VMEM((2, hidden // 256, total, 256), bf16),
            pltpu.VMEM((OUT_PARTS, total, nw), bf16),
            pltpu.VMEM((OUT_PARTS, NP, 2 * slots, nw), bf16),
            pltpu.VMEM((OUT_PARTS, NZ, 2 * rows, nw), f32),
            pltpu.VMEM((OUT_PARTS, NZ, 2 * rows, nw), bf16),
            pltpu.VMEM((OUT_PARTS, NZ, 2 * rows, nw), bf16),
            pltpu.VMEM((OUT_PARTS, NZ, 2 * rows, nw), bf16),
            pltpu.VMEM((OUT_PARTS, rows, nw), f32),
            pltpu.VMEM((OUT_PARTS, rows, nw), f32),
            dma((10,)),
            dma((4,)),
            dma((4,)),
            dma((NZ,)),
            dma((NZ,)),
            dma((2, IN_PARTS, NZ)),
            dma((IN_PARTS, NZ)),
            dma((IN_PARTS, NP)),
            dma((IN_PARTS, NP)),
            dma((IN_PARTS, NP)),
            dma((IN_PARTS, NP)),
            dma((hidden // 256,)),
            dma((hidden // 256,)),
            dma((OUT_PARTS, NP)),
            dma((OUT_PARTS, NP)),
            dma((OUT_PARTS, NZ)),
            dma((OUT_PARTS, NZ)),
            dma((OUT_PARTS, NZ)),
            dma((OUT_PARTS, NZ)),
            dma((half // 256,)),
            dma((half // 256,)),
            dma((OUT_PARTS,)),
            dma((OUT_PARTS,)),
        ],
        compiler_params=pltpu.CompilerParams(
            collective_id=0, has_side_effects=True, vmem_limit_bytes=62 * 1024 * 1024
        ),
    )(
        attention_out,
        residual,
        pre_gain,
        routes.T,
        gate_prob.T,
        out_weight,
        gate_weight,
        up_weight,
        down_weight,
    )
    return pl.pallas_call(
        end_kernel,
        out_shape=(
            jax.ShapeDtypeStruct((rows, width), bf16),
            jax.ShapeDtypeStruct((rows, width), bf16),
        ),
        in_specs=[vmem, vmem, hbm],
        out_specs=(vmem, vmem),
        scratch_shapes=[pltpu.VMEM((1, width), f32), dma(())],
    )(summed, expert_sum, post_gain)


def per_device(chips, *arrays):
    if chips == NZ * NP:
        return fused(*arrays)
    return routed_by_collectives(*arrays)


def solution(mesh):
    return jax.shard_map(
        functools.partial(per_device, mesh.shape["ep"]),
        mesh=mesh,
        in_specs=(
            P(("ep", "dp"), None),
            P(("ep", "dp"), None),
            P(None, "dp"),
            P(),
            P(("ep", "dp"), None),
            P(("ep", "dp"), None),
            P("ep", None, "dp"),
            P("ep", None, "dp"),
            P("ep", None, "dp"),
            P(),
        ),
        out_specs=(P(("ep", "dp"), None), P(("ep", "dp"), None)),
        check_vma=False,
    )
```
